32 devices in a mesh: site: 4 (over z), dev: 8 (over y, x, core).
Axes of the slice: x: 2, y: 2, z: 4, core: 2. Of those that a mesh axis runs over, the one named last changes fastest.
Arguments:
- tokens: bfloat16 [4, 1024, 8192], P('site', 'dev'), may hold values from -6 to 6
- cotangent: bfloat16 [4, 1024, 64], P('site', 'dev'), may hold values from -0.119628906 to 0.119628906
- weight: bfloat16 [64, 8192], P('dev'), may hold values from -0.0625 to 0.0625
- momentum: float32 [4, 64, 8192], P('site', 'dev'), may hold values from -6 to 6
- kept_index: int32 [4, 64, 128, 16], P(None, 'dev'), may hold values from 0 to 63, all different within a row
Outputs:
- scores: bfloat16 [4, 1024, 64], P('site', 'dev')
- momentum_out: float32 [4, 64, 8192], P('site', 'dev')
The draws below stay inside these ranges and needn't reach their ends.
Inputs may be any that keep to these rules, and one draw needn't show every extreme that they name: `kept_index`: the 16 indices of one block and site are all different.
All inputs are finite; a program needn't handle non-finite values.
Results may differ from the reference program's by a relative error of at most 0.022.
Values may be sent and summed in bfloat16 or wider, within the bound.
A program may use at most 64 MiB of HBM per device.

```python
import jax
import jax.numpy as jnp
from jax import lax

C = 8192
SPAN = 64
K = 16
TOK_DEV = 128
SITES = 4
ROWS = 64
TOKENS = 1024
BLOCKS = 128
N_DEV = 8


def steps_of(own_key, dims, split, least, top_value):
    factor_of = 1.0
    for position, blocks in split:
        draws = jax.random.uniform(jax.random.fold_in(jax.random.fold_in(own_key, 6), position), (blocks,), jnp.float32, least / len(split), top_value / len(split))
        factor_of = factor_of * jnp.repeat(jnp.exp(draws), dims[position] // blocks).reshape((-1,) + (1,) * (len(dims) - 1 - position))
    return factor_of


def picks_of(rng, rows, amount, top, lift):
    sequence = jax.random.permutation(jax.random.fold_in(rng, 1), amount)
    pull = sequence
    for power in range(3):
        pull = pull * pull // amount
    pull = pull * lift // amount
    lots = jax.random.randint(jax.random.fold_in(rng, 2), (rows, amount), 0, 4096) + pull
    holders = jax.random.permutation(jax.random.fold_in(rng, 3), rows)[jnp.arange(amount) % rows]
    lots = jnp.where(jnp.arange(rows)[:, None] == holders[None, :], 1 << 14, lots)
    score = lots * amount + jnp.arange(amount)
    return lax.top_k(score.astype(jnp.int32), top)[1].astype(jnp.int32)


def bell_draw(own_key, dims, width, bound, shards=(), held_as=jnp.bfloat16):
    entries = width * jax.random.normal(own_key, dims, jnp.float32)
    if shards:
        entries = entries * steps_of(own_key, dims, shards, -0.22, 0.18)
    return jnp.clip(entries, -bound, bound).astype(held_as)


def setup_inputs(seed: int = 0) -> dict:
    seeds = jax.random.split(jax.random.key(seed), 6)
    tokens = bell_draw(seeds[0], (SITES, TOKENS, C), 1.0, 6.0, ((0, 4), (1, 8)))
    cotangent = bell_draw(seeds[1], (SITES, TOKENS, ROWS), 0.02, 0.119628906, ((0, 4), (1, 8)))
    weight = bell_draw(seeds[2], (ROWS, C), C ** -0.5, 0.0625, ((0, 8),))
    momentum = bell_draw(seeds[3], (SITES, ROWS, C), 1.0, 6.0, ((0, 4), (1, 8)), jnp.float32)
    kept_index = picks_of(seeds[4], SITES * ROWS * BLOCKS, SPAN, K, 0).reshape((SITES, ROWS, BLOCKS, K))
    return {"tokens": tokens, "cotangent": cotangent, "weight": weight, "momentum": momentum, "kept_index": kept_index}


momentum_decay = 0.999
step_size = 0.01

def dct_table():
    freq = jnp.arange(64)[:, None].astype(jnp.float32)
    place = jnp.arange(64)[None, :].astype(jnp.float32)
    factor = jnp.where(freq == 0.0, jnp.sqrt(1.0 / 64.0), jnp.sqrt(2.0 / 64.0)).astype(jnp.float32)
    return (factor * jnp.cos(jnp.pi * (2.0 * place + 1.0) * freq / 128.0)).astype(jnp.float32)

def forward_dct(field, table):
    blocks = field.reshape(field.shape[0], -1, 64)
    return jnp.einsum('rcn,kn->rck', blocks, table, precision=lax.Precision.HIGHEST)

def inverse_dct(coefs, table):
    blocks = jnp.einsum('rck,kn->rcn', coefs, table, precision=lax.Precision.HIGHEST)
    return blocks.reshape(coefs.shape[0], -1)

def reference(tokens, cotangent, weight, momentum, kept_index):
    table = dct_table()
    iota_block = jnp.arange(64).astype(jnp.int32)

    def site_step(running, inputs):
        site_tokens, site_cotan, site_moment, site_index = inputs
        token_groups = site_tokens.reshape(N_DEV, TOK_DEV, C)
        cotan_groups = site_cotan.reshape(N_DEV, TOK_DEV, ROWS)

        def add_term(group, accum):
            term = lax.dot_general(cotan_groups[group], token_groups[group], (((0,), (0,)), ((), ())), preferred_element_type=jnp.float32)
            rounded = lax.optimization_barrier(term.astype(jnp.bfloat16))
            return accum + rounded.astype(jnp.float32)
        grad = lax.fori_loop(0, N_DEV, add_term, jnp.zeros((ROWS, C), jnp.float32))
        raised = momentum_decay * site_moment + grad
        coefs = forward_dct(raised, table)
        keep_mask = jnp.any(site_index[..., None] == iota_block, axis=2).astype(jnp.float32)
        picked = coefs * keep_mask
        moment_new = raised - inverse_dct(picked, table)
        sent = lax.optimization_barrier(picked.astype(jnp.bfloat16))
        return (running + sent.astype(jnp.float32), moment_new)
    zero_total = jnp.zeros((ROWS, C // 64, 64), jnp.float32)
    total, momentum_out = lax.scan(site_step, zero_total, (tokens, cotangent, momentum, kept_index))
    decoded = inverse_dct(total, table)
    new_weight = (weight.astype(jnp.float32) - step_size * decoded).astype(jnp.bfloat16)

    def project(site_tokens):
        return lax.dot_general(site_tokens, new_weight, (((1,), (1,)), ((), ())), preferred_element_type=jnp.float32).astype(jnp.bfloat16)
    scores = lax.map(project, tokens)
    return (scores, momentum_out)
```

```python
import functools

import jax
import jax.numpy as jnp
import ml_dtypes
import numpy as np
from jax import lax
from jax.experimental import pallas as pl
from jax.experimental.pallas import tpu as pltpu
from jax.sharding import PartitionSpec as P

momentum_decay = 0.999
step_size = 0.01
SPAN = 64
LANES = 128
CHUNKS = 4
MESH = pl.DeviceIdType.MESH
f32 = jnp.float32
bf16 = jnp.bfloat16


def split_table(table):
    high = table.astype(ml_dtypes.bfloat16)
    low = (table - high.astype(np.float64)).astype(ml_dtypes.bfloat16)
    return np.concatenate([high, high, low], axis=0)


def pair_tables():
    freq = np.arange(SPAN)[:, None]
    place = np.arange(SPAN)[None, :]
    factor = np.where(freq == 0, np.sqrt(1.0 / SPAN), np.sqrt(2.0 / SPAN))
    one = factor * np.cos(np.pi * (2 * place + 1) * freq / (2 * SPAN))
    pair = np.kron(np.eye(LANES // SPAN), one)
    return split_table(pair.T), split_table(pair)


def split_dot(field, factor):
    high = field.astype(bf16)
    low = (field - high.astype(f32)).astype(bf16)
    return jnp.dot(jnp.concatenate([high, low, high], axis=1), factor, preferred_element_type=f32)


def stack(field):
    return jnp.concatenate(
        [field[:, t * LANES:(t + 1) * LANES] for t in range(field.shape[1] // LANES)], axis=0
    )


def unstack(field, rows):
    return jnp.concatenate(
        [field[t * rows:(t + 1) * rows] for t in range(field.shape[0] // rows)], axis=1
    )


def flip_bits(index, bits):
    for power in range(bits.bit_length()):
        if (bits >> power) & 1:
            one = 1 << power
            index = index + one - 2 * one * ((index // one) % 2)
    return index


def kernel(
    n_dev, n_site,
    tok_hbm, cotan, weight, mom_hbm, index_hbm, forward, inverse,
    score_out, mom_out_hbm,
    tok, mom, index, mask, mom_new, terms, from_mate, chip_sum, from_chip, sent, from_site, new_rows,
    tok_sem, mom_sem, index_sem, out_sem,
    mate_send, mate_recv, chip_send, chip_recv, site_send, site_recv,
    row_send, row_recv, pass_send, pass_recv,
):
    chips = n_dev // 2
    rows, width = mom.shape
    span = width // CHUNKS
    tiles = span // LANES
    me = lax.axis_index("dev")
    site = lax.axis_index("site")
    chip, core = me // 2, me % 2
    mate = chip * 2 + 1 - core
    order = range(chips - 1, 0, -1)

    def peer(k):
        return flip_bits(chip, k) * 2 + core

    def other_site(k):
        return (site + k) % n_site

    barrier = pltpu.get_barrier_semaphore()
    pl.semaphore_signal(barrier, inc=1, device_id={"dev": mate}, device_id_type=MESH)
    for k in order:
        pl.semaphore_signal(barrier, inc=1, device_id={"dev": peer(k)}, device_id_type=MESH)
    for k in range(1, n_site):
        pl.semaphore_signal(barrier, inc=1, device_id={"site": other_site(k)}, device_id_type=MESH)

    def cols(q):
        return slice(q * span, (q + 1) * span)

    tok_loads = [
        pltpu.make_async_copy(tok_hbm.at[0, :, cols(q)], tok.at[:, cols(q)], tok_sem.at[q])
        for q in range(CHUNKS)
    ]
    for load in tok_loads:
        load.start()
    index_load = pltpu.make_async_copy(index_hbm.at[site], index, index_sem)
    index_load.start()
    mom_load = pltpu.make_async_copy(mom_hbm.at[0], mom, mom_sem)
    mom_load.start()

    def remote(src, dst, send_sem, recv_sem, **where):
        return pltpu.make_async_remote_copy(
            src_ref=src, dst_ref=dst, send_sem=send_sem, recv_sem=recv_sem,
            device_id=where, device_id_type=MESH,
        )

    def mate_copy(q):
        return remote(
            terms.at[1 - core, q], from_mate.at[q], mate_send.at[q], mate_recv.at[q], dev=mate
        )

    def chip_copy(q, k):
        return remote(
            chip_sum.at[q, flip_bits(chip, k)], from_chip.at[q, k - 1],
            chip_send.at[q, k - 1], chip_recv.at[q, k - 1], dev=peer(k),
        )

    def site_copy(q, k):
        return remote(
            sent.at[q], from_site.at[q, k - 1],
            site_send.at[q, k - 1], site_recv.at[q, k - 1], site=other_site(k),
        )

    def row_copy(q, k):
        to = mate if k == 0 else peer(k)
        return remote(
            new_rows.at[q, me], new_rows.at[q, me], row_send.at[q, k], row_recv.at[q, k], dev=to
        )

    def row_arrival(q, k):
        held = new_rows.at[q, mate if k == 0 else peer(k)]
        return remote(held, held, row_send.at[q, k], row_recv.at[q, k], dev=mate)

    def pass_copy(q, k):
        held = new_rows.at[q, peer(k)]
        return remote(held, held, pass_send.at[q, k - 1], pass_recv.at[q, k - 1], dev=mate)

    def pass_arrival(q, k):
        held = new_rows.at[q, flip_bits(chip, k) * 2 + 1 - core]
        return remote(held, held, pass_send.at[q, k - 1], pass_recv.at[q, k - 1], dev=mate)

    def multiply(q):
        tok_loads[q].wait()
        grad = jnp.dot(cotan[...], tok[:, cols(q)], preferred_element_type=f32)
        grad = grad.reshape(chips, 2, rows, span)
        for c in range(2):
            part = grad[:, c]
            part = jnp.concatenate(
                [part[:, :, t * LANES:(t + 1) * LANES] for t in range(tiles)], axis=1
            )
            terms[c, q] = part.astype(bf16)
        if q == 0:
            pl.semaphore_wait(barrier, chips + n_site - 1)
        mate_copy(q).start()

    def add_mate(q):
        mate_copy(q).wait_recv()
        both = terms[core, q].astype(f32) + from_mate[q].astype(f32)
        chip_sum[q] = both.astype(bf16)
        for k in order:
            chip_copy(q, k).start()

    def make_mask():
        index_load.wait()
        held = index[...]
        one = jnp.int32(1)
        low = jnp.sum(jnp.where(held < 32, one << (held & 31), 0), axis=1)
        high = jnp.sum(jnp.where(held >= 32, one << (held & 31), 0), axis=1)
        lane = lax.broadcasted_iota(jnp.int32, (rows, LANES), 1)
        first = lane < SPAN
        lower = (lane % SPAN) < 32
        shift = lane % 32
        for t in range(width // LANES):
            def word(block):
                return jnp.where(
                    lower,
                    jnp.broadcast_to(low[:, block:block + 1], (rows, LANES)),
                    jnp.broadcast_to(high[:, block:block + 1], (rows, LANES)),
                )
            words = jnp.where(first, word(2 * t), word(2 * t + 1))
            mask[t * rows:(t + 1) * rows, :] = ((words >> shift) & 1).astype(f32)

    def pick(q):
        if q == 0:
            mom_load.wait()
        for k in order:
            chip_copy(q, k).wait_recv()
        grad = terms[core, q, chip].astype(f32) + from_mate[q, chip].astype(f32)
        for k in order:
            grad = grad + from_chip[q, k - 1].astype(f32)
        raised = momentum_decay * stack(mom[:, cols(q)]) + grad
        picked = split_dot(raised, forward[...]) * mask[q * tiles * rows:(q + 1) * tiles * rows, :]
        sent[q] = picked.astype(bf16)
        for k in range(1, n_site):
            site_copy(q, k).start()
        kept = raised - split_dot(picked, inverse[...])
        mom_new[:, cols(q)] = unstack(kept, rows)
        mom_store(q).start()

    def mom_store(q):
        return pltpu.make_async_copy(
            mom_new.at[:, cols(q)], mom_out_hbm.at[0, :, cols(q)], out_sem.at[q]
        )

    def update(q):
        for k in range(1, n_site):
            site_copy(q, k).wait_recv()
        total = sent[q].astype(f32)
        for k in range(1, n_site):
            total = total + from_site[q, k - 1].astype(f32)
        decoded = split_dot(total, inverse[...])
        new_rows[q, me] = (
            stack(weight[:, cols(q)].astype(f32)) - step_size * decoded
        ).astype(bf16)
        for k in order:
            row_copy(q, k).start()
        row_copy(q, 0).start()

    def hand_on(q):
        for k in range(1, chips):
            row_arrival(q, k).wait_recv()
            pass_copy(q, k).start()

    def project(q, scores):
        row_arrival(q, 0).wait_recv()
        for k in range(1, chips):
            pass_arrival(q, k).wait_recv()
        held = new_rows[q].astype(f32)
        held = jnp.concatenate(
            [held[:, t * rows:(t + 1) * rows, :].reshape(n_dev * rows, LANES) for t in range(tiles)],
            axis=1,
        ).astype(bf16)
        return scores + lax.dot_general(
            held, tok[:, cols(q)], (((1,), (1,)), ((), ())), preferred_element_type=f32
        )

    scores = jnp.zeros(score_out.shape[1:], f32)
    for step in range(CHUNKS + 5):
        if step == 2:
            make_mask()
        for stage, shift in ((multiply, 0), (add_mate, 1), (pick, 2), (update, 3), (hand_on, 4)):
            if 0 <= step - shift < CHUNKS:
                stage(step - shift)
        if 0 <= step - 5 < CHUNKS:
            scores = project(step - 5, scores)
    score_out[0] = scores.astype(bf16)

    for q in range(CHUNKS):
        mate_copy(q).wait_send()
        for k in range(1, chips):
            chip_copy(q, k).wait_send()
            row_copy(q, k).wait_send()
            pass_copy(q, k).wait_send()
        row_copy(q, 0).wait_send()
        for k in range(1, n_site):
            site_copy(q, k).wait_send()
        mom_store(q).wait()


def shards(n_dev, n_site, tokens, cotangent, weight, momentum, kept_index):
    count, width = tokens.shape[1:]
    out_rows = cotangent.shape[2]
    rows = weight.shape[0]
    chips = n_dev // 2
    high = rows * width // LANES // CHUNKS
    forward, inverse = pair_tables()
    vmem = pl.BlockSpec(memory_space=pltpu.VMEM)
    anywhere = pl.BlockSpec(memory_space=pl.ANY)
    sems = pltpu.SemaphoreType.DMA
    kept = kept_index.shape[3]
    scores, momentum_new = pl.pallas_call(
        functools.partial(kernel, n_dev, n_site),
        out_shape=(
            jax.ShapeDtypeStruct((1, out_rows, count), bf16),
            jax.ShapeDtypeStruct(momentum.shape, f32),
        ),
        in_specs=[anywhere, vmem, vmem, anywhere, anywhere, vmem, vmem],
        out_specs=(vmem, anywhere),
        scratch_shapes=[
            pltpu.VMEM((count, width), bf16),
            pltpu.VMEM((rows, width), f32),
            pltpu.VMEM((rows, kept, width // SPAN), jnp.int32),
            pltpu.VMEM((high * CHUNKS, LANES), f32),
            pltpu.VMEM((rows, width), f32),
            pltpu.VMEM((2, CHUNKS, chips, high, LANES), bf16),
            pltpu.VMEM((CHUNKS, chips, high, LANES), bf16),
            pltpu.VMEM((CHUNKS, chips, high, LANES), bf16),
            pltpu.VMEM((CHUNKS, chips - 1, high, LANES), bf16),
            pltpu.VMEM((CHUNKS, high, LANES), bf16),
            pltpu.VMEM((CHUNKS, n_site - 1, high, LANES), bf16),
            pltpu.VMEM((CHUNKS, n_dev, high, LANES), bf16),
            sems((CHUNKS,)), sems, sems, sems((CHUNKS,)),
            sems((CHUNKS,)), sems((CHUNKS,)),
            sems((CHUNKS, chips - 1)), sems((CHUNKS, chips - 1)),
            sems((CHUNKS, n_site - 1)), sems((CHUNKS, n_site - 1)),
            sems((CHUNKS, chips)), sems((CHUNKS, chips)),
            sems((CHUNKS, chips - 1)), sems((CHUNKS, chips - 1)),
        ],
        compiler_params=pltpu.CompilerParams(
            collective_id=0, has_side_effects=True, vmem_limit_bytes=50 * 1024 * 1024
        ),
        cost_estimate=pl.CostEstimate(
            flops=4 * count * width * out_rows, bytes_accessed=4 * count * width, transcendentals=0
        ),
    )(
        tokens,
        cotangent[0].T,
        weight,
        momentum,
        kept_index.transpose(0, 1, 3, 2),
        jnp.asarray(forward),
        jnp.asarray(inverse),
    )
    return scores.transpose(0, 2, 1), momentum_new


def solution(mesh):
    placed = (
        P("site", "dev", None),
        P("site", "dev", None),
        P("dev", None),
        P("site", "dev", None),
        P(None, "dev", None, None),
    )
    return jax.shard_map(
        functools.partial(shards, mesh.shape["dev"], mesh.shape["site"]),
        mesh=mesh,
        in_specs=placed,
        out_specs=(P("site", "dev", None), P("site", "dev", None)),
        check_vma=False,
    )
```

```python
import functools

import jax
import jax.numpy as jnp
import ml_dtypes
import numpy as np
from jax import lax
from jax.experimental import pallas as pl
from jax.experimental.pallas import tpu as pltpu
from jax.sharding import PartitionSpec as P

momentum_decay = 0.999
step_size = 0.01
SPAN = 64
LANES = 128
CHUNKS = 4
MESH = pl.DeviceIdType.MESH
f32 = jnp.float32
bf16 = jnp.bfloat16


def split_table(table):
    high = table.astype(ml_dtypes.bfloat16)
    low = (table - high.astype(np.float64)).astype(ml_dtypes.bfloat16)
    return np.concatenate([high, high, low], axis=0)


def pair_tables():
    freq = np.arange(SPAN)[:, None]
    place = np.arange(SPAN)[None, :]
    factor = np.where(freq == 0, np.sqrt(1.0 / SPAN), np.sqrt(2.0 / SPAN))
    one = factor * np.cos(np.pi * (2 * place + 1) * freq / (2 * SPAN))
    pair = np.kron(np.eye(LANES // SPAN), one)
    return np.stack([split_table(pair.T), split_table(pair)])


def split_dot(field, factor):
    high = field.astype(bf16)
    low = (field - high.astype(f32)).astype(bf16)
    return jnp.dot(jnp.concatenate([high, low, high], axis=1), factor, preferred_element_type=f32)


def stack(field):
    return jnp.concatenate(
        [field[:, t * LANES:(t + 1) * LANES] for t in range(field.shape[1] // LANES)], axis=0
    )


def unstack(field, rows):
    return jnp.concatenate(
        [field[t * rows:(t + 1) * rows] for t in range(field.shape[0] // rows)], axis=1
    )


def flip_bits(index, bits):
    for power in range(bits.bit_length()):
        if (bits >> power) & 1:
            one = 1 << power
            index = index + one - 2 * one * ((index // one) % 2)
    return index


def kernel(
    n_dev, n_site,
    tok_hbm, cotan_hbm, weight_hbm, mom_hbm, index_hbm, table_hbm,
    score_out, mom_out_hbm,
    cotan, weight, table, tok, mom, index, mask, mom_new, terms, from_mate, chip_sum, from_chip, sent, from_site, new_rows,
    cotan_sem, weight_sem, table_sem, tok_sem, mom_sem, index_sem, out_sem,
    mate_send, mate_recv, chip_send, chip_recv, site_send, site_recv,
    row_send, row_recv, pass_send, pass_recv,
):
    chips = n_dev // 2
    rows, width = mom.shape
    span = width // CHUNKS
    tiles = span // LANES
    me = lax.axis_index("dev")
    site = lax.axis_index("site")
    chip, core = me // 2, me % 2
    mate = chip * 2 + 1 - core
    order = range(chips - 1, 0, -1)

    def peer(k):
        return flip_bits(chip, k) * 2 + core

    def other_site(k):
        return (site + k) % n_site

    barrier = pltpu.get_barrier_semaphore()
    pl.semaphore_signal(barrier, inc=1, device_id={"dev": mate}, device_id_type=MESH)
    for k in order:
        pl.semaphore_signal(barrier, inc=1, device_id={"dev": peer(k)}, device_id_type=MESH)
    for k in range(1, n_site):
        pl.semaphore_signal(barrier, inc=1, device_id={"site": other_site(k)}, device_id_type=MESH)

    def cols(q):
        return slice(q * span, (q + 1) * span)

    tok_loads = [
        pltpu.make_async_copy(tok_hbm.at[0, :, cols(q)], tok.at[:, cols(q)], tok_sem.at[q])
        for q in range(CHUNKS)
    ]
    cotan_load = pltpu.make_async_copy(cotan_hbm, cotan, cotan_sem)
    weight_load = pltpu.make_async_copy(weight_hbm, weight, weight_sem)
    table_load = pltpu.make_async_copy(table_hbm, table, table_sem)
    cotan_load.start()
    for load in tok_loads:
        load.start()
    index_load = pltpu.make_async_copy(index_hbm.at[site], index, index_sem)
    index_load.start()
    mom_load = pltpu.make_async_copy(mom_hbm.at[0], mom, mom_sem)
    mom_load.start()
    table_load.start()
    weight_load.start()

    def remote(src, dst, send_sem, recv_sem, **where):
        return pltpu.make_async_remote_copy(
            src_ref=src, dst_ref=dst, send_sem=send_sem, recv_sem=recv_sem,
            device_id=where, device_id_type=MESH,
        )

    def mate_copy(q):
        return remote(
            terms.at[1 - core, q], from_mate.at[q], mate_send.at[q], mate_recv.at[q], dev=mate
        )

    def chip_copy(q, k):
        return remote(
            chip_sum.at[q, flip_bits(chip, k)], from_chip.at[q, k - 1],
            chip_send.at[q, k - 1], chip_recv.at[q, k - 1], dev=peer(k),
        )

    def site_copy(q, k):
        return remote(
            sent.at[q], from_site.at[q, k - 1],
            site_send.at[q, k - 1], site_recv.at[q, k - 1], site=other_site(k),
        )

    def row_copy(q, k):
        to = mate if k == 0 else peer(k)
        return remote(
            new_rows.at[q, me], new_rows.at[q, me], row_send.at[q, k], row_recv.at[q, k], dev=to
        )

    def row_arrival(q, k):
        held = new_rows.at[q, mate if k == 0 else peer(k)]
        return remote(held, held, row_send.at[q, k], row_recv.at[q, k], dev=mate)

    def pass_copy(q, k):
        held = new_rows.at[q, peer(k)]
        return remote(held, held, pass_send.at[q, k - 1], pass_recv.at[q, k - 1], dev=mate)

    def pass_arrival(q, k):
        held = new_rows.at[q, flip_bits(chip, k) * 2 + 1 - core]
        return remote(held, held, pass_send.at[q, k - 1], pass_recv.at[q, k - 1], dev=mate)

    def multiply(q):
        if q == 0:
            cotan_load.wait()
        tok_loads[q].wait()
        grad = jnp.dot(cotan[...], tok[:, cols(q)], preferred_element_type=f32)
        grad = grad.reshape(chips, 2, rows, span)
        for c in range(2):
            part = grad[:, c]
            part = jnp.concatenate(
                [part[:, :, t * LANES:(t + 1) * LANES] for t in range(tiles)], axis=1
            )
            terms[c, q] = part.astype(bf16)
        if q == 0:
            pl.semaphore_wait(barrier, chips + n_site - 1)
        mate_copy(q).start()

    def add_mate(q):
        mate_copy(q).wait_recv()
        both = terms[core, q].astype(f32) + from_mate[q].astype(f32)
        chip_sum[q] = both.astype(bf16)
        for k in order:
            chip_copy(q, k).start()

    def make_mask():
        index_load.wait()
        held = index[...]
        one = jnp.int32(1)
        low = jnp.sum(jnp.where(held < 32, one << (held & 31), 0), axis=1)
        high = jnp.sum(jnp.where(held >= 32, one << (held & 31), 0), axis=1)
        lane = lax.broadcasted_iota(jnp.int32, (rows, LANES), 1)
        first = lane < SPAN
        lower = (lane % SPAN) < 32
        shift = lane % 32
        for t in range(width // LANES):
            def word(block):
                return jnp.where(
                    lower,
                    jnp.broadcast_to(low[:, block:block + 1], (rows, LANES)),
                    jnp.broadcast_to(high[:, block:block + 1], (rows, LANES)),
                )
            words = jnp.where(first, word(2 * t), word(2 * t + 1))
            mask[t * rows:(t + 1) * rows, :] = ((words >> shift) & 1).astype(f32)

    def pick(q):
        if q == 0:
            mom_load.wait()
            table_load.wait()
        for k in order:
            chip_copy(q, k).wait_recv()
        grad = terms[core, q, chip].astype(f32) + from_mate[q, chip].astype(f32)
        for k in order:
            grad = grad + from_chip[q, k - 1].astype(f32)
        raised = momentum_decay * stack(mom[:, cols(q)]) + grad
        picked = split_dot(raised, table[0]) * mask[q * tiles * rows:(q + 1) * tiles * rows, :]
        sent[q] = picked.astype(bf16)
        for k in range(1, n_site):
            site_copy(q, k).start()
        kept = raised - split_dot(picked, table[1])
        mom_new[:, cols(q)] = unstack(kept, rows)
        mom_store(q).start()

    def mom_store(q):
        return pltpu.make_async_copy(
            mom_new.at[:, cols(q)], mom_out_hbm.at[0, :, cols(q)], out_sem.at[q]
        )

    def update(q):
        for k in range(1, n_site):
            site_copy(q, k).wait_recv()
        if q == 0:
            weight_load.wait()
        total = sent[q].astype(f32)
        for k in range(1, n_site):
            total = total + from_site[q, k - 1].astype(f32)
        decoded = split_dot(total, table[1])
        new_rows[q, me] = (
            stack(weight[:, cols(q)].astype(f32)) - step_size * decoded
        ).astype(bf16)
        for k in order:
            row_copy(q, k).start()
        row_copy(q, 0).start()

    def hand_on(q):
        for k in range(1, chips):
            row_arrival(q, k).wait_recv()
            pass_copy(q, k).start()

    def project(q, scores):
        row_arrival(q, 0).wait_recv()
        for k in range(1, chips):
            pass_arrival(q, k).wait_recv()
        held = new_rows[q].astype(f32)
        held = jnp.concatenate(
            [held[:, t * rows:(t + 1) * rows, :].reshape(n_dev * rows, LANES) for t in range(tiles)],
            axis=1,
        ).astype(bf16)
        return scores + lax.dot_general(
            held, tok[:, cols(q)], (((1,), (1,)), ((), ())), preferred_element_type=f32
        )

    scores = jnp.zeros(score_out.shape[1:], f32)
    for q in range(CHUNKS):
        multiply(q)
    for q in range(CHUNKS):
        add_mate(q)
    make_mask()
    for step in range(CHUNKS + 5):
        if step < CHUNKS:
            pick(step)
        for stage, shift in ((update, 2), (hand_on, 4)):
            if 0 <= step - shift < CHUNKS:
                stage(step - shift)
        if 0 <= step - 5 < CHUNKS:
            scores = project(step - 5, scores)
    score_out[0] = scores.astype(bf16)

    for q in range(CHUNKS):
        mate_copy(q).wait_send()
        for k in range(1, chips):
            chip_copy(q, k).wait_send()
            row_copy(q, k).wait_send()
            pass_copy(q, k).wait_send()
        row_copy(q, 0).wait_send()
        for k in range(1, n_site):
            site_copy(q, k).wait_send()
        mom_store(q).wait()


def shards(n_dev, n_site, tokens, cotangent, weight, momentum, kept_index):
    count, width = tokens.shape[1:]
    out_rows = cotangent.shape[2]
    rows = weight.shape[0]
    chips = n_dev // 2
    high = rows * width // LANES // CHUNKS
    tables = pair_tables()
    vmem = pl.BlockSpec(memory_space=pltpu.VMEM)
    hbm = pl.BlockSpec(memory_space=pltpu.HBM)
    sems = pltpu.SemaphoreType.DMA
    kept = kept_index.shape[3]
    scores, momentum_new = pl.pallas_call(
        functools.partial(kernel, n_dev, n_site),
        out_shape=(
            jax.ShapeDtypeStruct((1, out_rows, count), bf16),
            jax.ShapeDtypeStruct(momentum.shape, f32),
        ),
        in_specs=[hbm] * 6,
        out_specs=(vmem, hbm),
        scratch_shapes=[
            pltpu.VMEM((out_rows, count), bf16),
            pltpu.VMEM((rows, width), bf16),
            pltpu.VMEM(tables.shape, bf16),
            pltpu.VMEM((count, width), bf16),
            pltpu.VMEM((rows, width), f32),
            pltpu.VMEM((rows, kept, width // SPAN), jnp.int32),
            pltpu.VMEM((high * CHUNKS, LANES), f32),
            pltpu.VMEM((rows, width), f32),
            pltpu.VMEM((2, CHUNKS, chips, high, LANES), bf16),
            pltpu.VMEM((CHUNKS, chips, high, LANES), bf16),
            pltpu.VMEM((CHUNKS, chips, high, LANES), bf16),
            pltpu.VMEM((CHUNKS, chips - 1, high, LANES), bf16),
            pltpu.VMEM((CHUNKS, high, LANES), bf16),
            pltpu.VMEM((CHUNKS, n_site - 1, high, LANES), bf16),
            pltpu.VMEM((CHUNKS, n_dev, high, LANES), bf16),
            sems, sems, sems, sems((CHUNKS,)), sems, sems, sems((CHUNKS,)),
            sems((CHUNKS,)), sems((CHUNKS,)),
            sems((CHUNKS, chips - 1)), sems((CHUNKS, chips - 1)),
            sems((CHUNKS, n_site - 1)), sems((CHUNKS, n_site - 1)),
            sems((CHUNKS, chips)), sems((CHUNKS, chips)),
            sems((CHUNKS, chips - 1)), sems((CHUNKS, chips - 1)),
        ],
        compiler_params=pltpu.CompilerParams(
            collective_id=0, has_side_effects=True, vmem_limit_bytes=56 * 1024 * 1024
        ),
        cost_estimate=pl.CostEstimate(
            flops=4 * count * width * out_rows, bytes_accessed=4 * count * width, transcendentals=0
        ),
    )(
        tokens,
        cotangent[0].T,
        weight,
        momentum,
        kept_index.transpose(0, 1, 3, 2),
        jnp.asarray(tables),
    )
    return scores.transpose(0, 2, 1), momentum_new


def solution(mesh):
    placed = (
        P("site", "dev", None),
        P("site", "dev", None),
        P("dev", None),
        P("site", "dev", None),
        P(None, "dev", None, None),
    )
    return jax.shard_map(
        functools.partial(shards, mesh.shape["dev"], mesh.shape["site"]),
        mesh=mesh,
        in_specs=placed,
        out_specs=(P("site", "dev", None), P("site", "dev", None)),
        check_vma=False,
    )
```

```python
import functools

import jax
import jax.numpy as jnp
import ml_dtypes
import numpy as np
from jax import lax
from jax.experimental import pallas as pl
from jax.experimental.pallas import tpu as pltpu
from jax.sharding import PartitionSpec as P

momentum_decay = 0.999
step_size = 0.01
SPAN = 64
LANES = 128
MESH = pl.DeviceIdType.MESH
f32 = jnp.float32
bf16 = jnp.bfloat16


def split_table(table):
    high = table.astype(ml_dtypes.bfloat16)
    low = (table - high.astype(np.float64)).astype(ml_dtypes.bfloat16)
    return np.concatenate([high, high, low], axis=0)


def pair_tables():
    freq = np.arange(SPAN)[:, None]
    place = np.arange(SPAN)[None, :]
    factor = np.where(freq == 0, np.sqrt(1.0 / SPAN), np.sqrt(2.0 / SPAN))
    one = factor * np.cos(np.pi * (2 * place + 1) * freq / (2 * SPAN))
    pair = np.kron(np.eye(LANES // SPAN), one)
    return np.stack([split_table(pair.T), split_table(pair)])


def split_dot(field, factor):
    high = field.astype(bf16)
    low = (field - high.astype(f32)).astype(bf16)
    return jnp.dot(jnp.concatenate([high, low, high], axis=1), factor, preferred_element_type=f32)


def stack(field):
    return jnp.concatenate(
        [field[:, t * LANES:(t + 1) * LANES] for t in range(field.shape[1] // LANES)], axis=0
    )


def unstack(field, rows):
    return jnp.concatenate(
        [field[t * rows:(t + 1) * rows] for t in range(field.shape[0] // rows)], axis=1
    )


def flip_bits(index, bits):
    for power in range(bits.bit_length()):
        if (bits >> power) & 1:
            one = 1 << power
            index = index + one - 2 * one * ((index // one) % 2)
    return index


def kernel(
    n_dev, n_site, chunks,
    tok_hbm, cotan_hbm, weight_hbm, mom_hbm, index_hbm, table_hbm,
    score_out, mom_out,
    cotan, weight, table, tok, mom, index, mask, terms, from_mate, chip_sum, from_chip, sent, from_site, new_rows,
    cotan_sem, weight_sem, table_sem, tok_sem, mom_sem, index_sem,
    mate_send, mate_recv, chip_send, chip_recv, site_send, site_recv, share_send, share_recv,
    row_send, row_recv, pass_send, pass_recv,
):
    chips = n_dev // 2
    rows, width = mom.shape
    span = width // chunks
    tiles = span // LANES
    piece = tiles * rows // n_site
    me = lax.axis_index("dev")
    site = lax.axis_index("site")
    chip, core = me // 2, me % 2
    mate = chip * 2 + 1 - core
    order = range(chips - 1, 0, -1)

    def peer(k):
        return flip_bits(chip, k) * 2 + core

    def other_site(k):
        return (site + k) % n_site

    barrier = pltpu.get_barrier_semaphore()
    pl.semaphore_signal(barrier, inc=1, device_id={"dev": mate}, device_id_type=MESH)
    for k in order:
        pl.semaphore_signal(barrier, inc=1, device_id={"dev": peer(k)}, device_id_type=MESH)
    for k in range(1, n_site):
        pl.semaphore_signal(barrier, inc=1, device_id={"site": other_site(k)}, device_id_type=MESH)

    def piece_of(index):
        return pl.ds(pl.multiple_of(index * piece, piece), piece)

    def cols(q):
        return slice(q * span, (q + 1) * span)

    tok_loads = [
        pltpu.make_async_copy(tok_hbm.at[0, :, cols(q)], tok.at[:, cols(q)], tok_sem.at[q])
        for q in range(chunks)
    ]
    cotan_load = pltpu.make_async_copy(cotan_hbm, cotan, cotan_sem)
    weight_load = pltpu.make_async_copy(weight_hbm, weight, weight_sem)
    table_load = pltpu.make_async_copy(table_hbm, table, table_sem)
    cotan_load.start()
    for load in tok_loads:
        load.start()
    index_load = pltpu.make_async_copy(index_hbm.at[site], index, index_sem)
    index_load.start()
    mom_load = pltpu.make_async_copy(mom_hbm.at[0], mom, mom_sem)
    mom_load.start()
    table_load.start()
    weight_load.start()

    def remote(src, dst, send_sem, recv_sem, **where):
        return pltpu.make_async_remote_copy(
            src_ref=src, dst_ref=dst, send_sem=send_sem, recv_sem=recv_sem,
            device_id=where, device_id_type=MESH,
        )

    def mate_copy(q):
        return remote(
            terms.at[1 - core, q], from_mate.at[q], mate_send.at[q], mate_recv.at[q], dev=mate
        )

    def chip_copy(q, k):
        return remote(
            chip_sum.at[q, flip_bits(chip, k)], from_chip.at[q, k - 1],
            chip_send.at[q, k - 1], chip_recv.at[q, k - 1], dev=peer(k),
        )

    def site_copy(q, k):
        return remote(
            sent.at[q, piece_of(other_site(k))], from_site.at[q, k - 1],
            site_send.at[q, k - 1], site_recv.at[q, k - 1], site=other_site(k),
        )

    def share_copy(q, k):
        held = new_rows.at[q, me, piece_of(site)]
        return remote(
            held, held, share_send.at[q, k - 1], share_recv.at[q, k - 1], site=other_site(k)
        )

    def share_arrival(q, k):
        held = new_rows.at[q, me, piece_of((site + n_site - k) % n_site)]
        return remote(
            held, held, share_send.at[q, k - 1], share_recv.at[q, k - 1], site=other_site(k)
        )

    def row_copy(q, k):
        to = mate if k == 0 else peer(k)
        return remote(
            new_rows.at[q, me], new_rows.at[q, me], row_send.at[q, k], row_recv.at[q, k], dev=to
        )

    def row_arrival(q, k):
        held = new_rows.at[q, mate if k == 0 else peer(k)]
        return remote(held, held, row_send.at[q, k], row_recv.at[q, k], dev=mate)

    def pass_copy(q, k):
        held = new_rows.at[q, peer(k)]
        return remote(held, held, pass_send.at[q, k - 1], pass_recv.at[q, k - 1], dev=mate)

    def pass_arrival(q, k):
        held = new_rows.at[q, flip_bits(chip, k) * 2 + 1 - core]
        return remote(held, held, pass_send.at[q, k - 1], pass_recv.at[q, k - 1], dev=mate)

    def multiply(q):
        if q == 0:
            cotan_load.wait()
        tok_loads[q].wait()
        grad = jnp.dot(cotan[...], tok[:, cols(q)], preferred_element_type=f32)
        grad = grad.reshape(chips, 2, rows, span)
        for c in range(2):
            part = grad[:, c]
            part = jnp.concatenate(
                [part[:, :, t * LANES:(t + 1) * LANES] for t in range(tiles)], axis=1
            )
            terms[c, q] = part.astype(bf16)
        if q == 0:
            pl.semaphore_wait(barrier, chips + n_site - 1)
        mate_copy(q).start()

    def add_mate(q):
        mate_copy(q).wait_recv()
        both = terms[core, q].astype(f32) + from_mate[q].astype(f32)
        chip_sum[q] = both.astype(bf16)
        for k in order:
            chip_copy(q, k).start()

    def make_mask():
        index_load.wait()
        held = index[...]
        one = jnp.int32(1)
        low = jnp.sum(jnp.where(held < 32, one << (held & 31), 0), axis=1)
        high = jnp.sum(jnp.where(held >= 32, one << (held & 31), 0), axis=1)
        lane = lax.broadcasted_iota(jnp.int32, (rows, LANES), 1)
        first = lane < SPAN
        lower = (lane % SPAN) < 32
        shift = lane % 32
        for t in range(width // LANES):
            def word(block):
                return jnp.where(
                    lower,
                    jnp.broadcast_to(low[:, block:block + 1], (rows, LANES)),
                    jnp.broadcast_to(high[:, block:block + 1], (rows, LANES)),
                )
            words = jnp.where(first, word(2 * t), word(2 * t + 1))
            mask[t * rows:(t + 1) * rows, :] = ((words >> shift) & 1).astype(f32)

    def pick(q):
        if q == 0:
            mom_load.wait()
            table_load.wait()
        for k in order:
            chip_copy(q, k).wait_recv()
        grad = terms[core, q, chip].astype(f32) + from_mate[q, chip].astype(f32)
        for k in order:
            grad = grad + from_chip[q, k - 1].astype(f32)
        raised = momentum_decay * stack(mom[:, cols(q)]) + grad
        picked = split_dot(raised, table[0]) * mask[q * tiles * rows:(q + 1) * tiles * rows, :]
        sent[q] = picked.astype(bf16)
        for k in range(1, n_site):
            site_copy(q, k).start()
        kept = raised - split_dot(picked, table[1])
        mom_out[0, :, cols(q)] = unstack(kept, rows)

    def update(q):
        for k in range(1, n_site):
            site_copy(q, k).wait_recv()
        if q == 0:
            weight_load.wait()
        total = sent[q, piece_of(site)].astype(f32)
        for k in range(1, n_site):
            total = total + from_site[q, k - 1].astype(f32)
        decoded = split_dot(total, table[1])
        wide = span // n_site
        own = weight[:, pl.ds(pl.multiple_of(q * span + site * wide, wide), wide)]
        new_rows[q, me, piece_of(site)] = (
            stack(own.astype(f32)) - step_size * decoded
        ).astype(bf16)
        for k in range(1, n_site):
            share_copy(q, k).start()

    def spread(q):
        for k in range(1, n_site):
            share_arrival(q, k).wait_recv()
        for k in order:
            row_copy(q, k).start()
        row_copy(q, 0).start()

    def hand_on(q):
        for k in range(1, chips):
            row_arrival(q, k).wait_recv()
            pass_copy(q, k).start()

    def project(q, scores):
        row_arrival(q, 0).wait_recv()
        for k in range(1, chips):
            pass_arrival(q, k).wait_recv()
        held = new_rows[q].astype(f32)
        held = jnp.concatenate(
            [held[:, t * rows:(t + 1) * rows, :].reshape(n_dev * rows, LANES) for t in range(tiles)],
            axis=1,
        ).astype(bf16)
        return scores + lax.dot_general(
            held, tok[:, cols(q)], (((1,), (1,)), ((), ())), preferred_element_type=f32
        )

    scores = jnp.zeros(score_out.shape[1:], f32)
    for q in range(chunks):
        multiply(q)
    for q in range(chunks):
        add_mate(q)
    make_mask()
    for step in range(chunks + 6):
        if step < chunks:
            pick(step)
        for stage, shift in ((update, 1), (spread, 2), (hand_on, 4)):
            if 0 <= step - shift < chunks:
                stage(step - shift)
        if 0 <= step - 5 < chunks:
            scores = project(step - 5, scores)
    score_out[0] = scores.astype(bf16)

    for q in range(chunks):
        mate_copy(q).wait_send()
        for k in range(1, chips):
            chip_copy(q, k).wait_send()
            row_copy(q, k).wait_send()
            pass_copy(q, k).wait_send()
        row_copy(q, 0).wait_send()
        for k in range(1, n_site):
            site_copy(q, k).wait_send()
            share_copy(q, k).wait_send()


def shards(n_dev, n_site, tokens, cotangent, weight, momentum, kept_index):
    count, width = tokens.shape[1:]
    out_rows = cotangent.shape[2]
    rows = weight.shape[0]
    chips = n_dev // 2
    chunks = min(4, rows * width // LANES // (16 * n_site))
    high = rows * width // LANES // chunks
    tables = pair_tables()
    vmem = pl.BlockSpec(memory_space=pltpu.VMEM)
    hbm = pl.BlockSpec(memory_space=pltpu.HBM)
    sems = pltpu.SemaphoreType.DMA
    kept = kept_index.shape[3]
    scores, momentum_new = pl.pallas_call(
        functools.partial(kernel, n_dev, n_site, chunks),
        out_shape=(
            pltpu.VMEM((1, out_rows, count), bf16),
            pltpu.VMEM(momentum.shape, f32),
        ),
        in_specs=[hbm] * 6,
        out_specs=(vmem, vmem),
        scratch_shapes=[
            pltpu.VMEM((out_rows, count), bf16),
            pltpu.VMEM((rows, width), bf16),
            pltpu.VMEM(tables.shape, bf16),
            pltpu.VMEM((count, width), bf16),
            pltpu.VMEM((rows, width), f32),
            pltpu.VMEM((rows, kept, width // SPAN), jnp.int32),
            pltpu.VMEM((high * chunks, LANES), f32),
            pltpu.VMEM((2, chunks, chips, high, LANES), bf16),
            pltpu.VMEM((chunks, chips, high, LANES), bf16),
            pltpu.VMEM((chunks, chips, high, LANES), bf16),
            pltpu.VMEM((chunks, chips - 1, high, LANES), bf16),
            pltpu.VMEM((chunks, high, LANES), bf16),
            pltpu.VMEM((chunks, n_site - 1, high // n_site, LANES), bf16),
            pltpu.VMEM((chunks, n_dev, high, LANES), bf16),
            sems, sems, sems, sems((chunks,)), sems, sems,
            sems((chunks,)), sems((chunks,)),
            sems((chunks, chips - 1)), sems((chunks, chips - 1)),
            sems((chunks, n_site - 1)), sems((chunks, n_site - 1)),
            sems((chunks, n_site - 1)), sems((chunks, n_site - 1)),
            sems((chunks, chips)), sems((chunks, chips)),
            sems((chunks, chips - 1)), sems((chunks, chips - 1)),
        ],
        compiler_params=pltpu.CompilerParams(
            collective_id=0, has_side_effects=True, vmem_limit_bytes=56 * 1024 * 1024
        ),
        cost_estimate=pl.CostEstimate(
            flops=4 * count * width * out_rows, bytes_accessed=4 * count * width, transcendentals=0
        ),
    )(
        tokens,
        cotangent[0].T,
        weight,
        momentum,
        kept_index.transpose(0, 1, 3, 2),
        jnp.asarray(tables),
    )
    return scores.transpose(0, 2, 1), momentum_new


def solution(mesh):
    placed = (
        P("site", "dev", None),
        P("site", "dev", None),
        P("dev", None),
        P("site", "dev", None),
        P(None, "dev", None, None),
    )
    return jax.shard_map(
        functools.partial(shards, mesh.shape["dev"], mesh.shape["site"]),
        mesh=mesh,
        in_specs=placed,
        out_specs=(P("site", "dev", None), P("site", "dev", None)),
        check_vma=False,
    )
```

```python
import functools

import jax
import jax.numpy as jnp
import ml_dtypes
import numpy as np
from jax import lax
from jax.experimental import pallas as pl
from jax.experimental.pallas import tpu as pltpu
from jax.sharding import PartitionSpec as P

momentum_decay = 0.999
step_size = 0.01
SPAN = 64
LANES = 128
CHUNKS = 4
MESH = pl.DeviceIdType.MESH
f32 = jnp.float32
bf16 = jnp.bfloat16


def split_table(table):
    high = table.astype(ml_dtypes.bfloat16)
    low = (table - high.astype(np.float64)).astype(ml_dtypes.bfloat16)
    return np.concatenate([high, high, low], axis=0)


def pair_tables():
    freq = np.arange(SPAN)[:, None]
    place = np.arange(SPAN)[None, :]
    factor = np.where(freq == 0, np.sqrt(1.0 / SPAN), np.sqrt(2.0 / SPAN))
    one = factor * np.cos(np.pi * (2 * place + 1) * freq / (2 * SPAN))
    pair = np.kron(np.eye(LANES // SPAN), one)
    return np.stack([split_table(pair.T), split_table(pair)])


def split_dot(field, factor):
    high = field.astype(bf16)
    low = (field - high.astype(f32)).astype(bf16)
    return jnp.dot(jnp.concatenate([high, low, high], axis=1), factor, preferred_element_type=f32)


def stack(field):
    return jnp.concatenate(
        [field[:, t * LANES:(t + 1) * LANES] for t in range(field.shape[1] // LANES)], axis=0
    )


def unstack(field, rows):
    return jnp.concatenate(
        [field[t * rows:(t + 1) * rows] for t in range(field.shape[0] // rows)], axis=1
    )


def flip_bits(index, bits):
    for power in range(bits.bit_length()):
        if (bits >> power) & 1:
            one = 1 << power
            index = index + one - 2 * one * ((index // one) % 2)
    return index


def kernel(
    n_dev, n_site,
    tok_hbm, cotan_hbm, weight_hbm, mom_hbm, index_hbm, table_hbm,
    score_out, mom_out,
    cotan, weight, table, tok, mom, index, mask, total_scores, terms, from_mate, chip_sum, from_chip, sent, from_site, new_rows,
    cotan_sem, weight_sem, table_sem, tok_sem, mom_sem, index_sem,
    mate_send, mate_recv, chip_send, chip_recv, site_send, site_recv,
    row_send, row_recv, pass_send, pass_recv,
):
    chips = n_dev // 2
    rows, width = mom.shape
    span = width // CHUNKS
    tiles = span // LANES
    me = lax.axis_index("dev")
    site = lax.axis_index("site")
    chip, core = me // 2, me % 2
    mate = chip * 2 + 1 - core
    order = range(chips - 1, 0, -1)

    def peer(k):
        return flip_bits(chip, k) * 2 + core

    def other_site(k):
        return (site + k) % n_site

    barrier = pltpu.get_barrier_semaphore()
    pl.semaphore_signal(barrier, inc=1, device_id={"dev": mate}, device_id_type=MESH)
    for k in order:
        pl.semaphore_signal(barrier, inc=1, device_id={"dev": peer(k)}, device_id_type=MESH)
    for k in range(1, n_site):
        pl.semaphore_signal(barrier, inc=1, device_id={"site": other_site(k)}, device_id_type=MESH)

    def cols(q):
        return pl.ds(pl.multiple_of(q * span, span), span)

    def tok_load(q):
        return pltpu.make_async_copy(tok_hbm.at[0, :, cols(q)], tok.at[:, cols(q)], tok_sem.at[q])

    cotan_load = pltpu.make_async_copy(cotan_hbm, cotan, cotan_sem)
    weight_load = pltpu.make_async_copy(weight_hbm, weight, weight_sem)
    table_load = pltpu.make_async_copy(table_hbm, table, table_sem)
    cotan_load.start()
    for q in range(CHUNKS):
        tok_load(q).start()
    index_load = pltpu.make_async_copy(index_hbm.at[site], index, index_sem)
    index_load.start()
    mom_load = pltpu.make_async_copy(mom_hbm.at[0], mom, mom_sem)
    mom_load.start()
    table_load.start()
    weight_load.start()

    def remote(src, dst, send_sem, recv_sem, **where):
        return pltpu.make_async_remote_copy(
            src_ref=src, dst_ref=dst, send_sem=send_sem, recv_sem=recv_sem,
            device_id=where, device_id_type=MESH,
        )

    def mate_copy(q):
        return remote(
            terms.at[1 - core, q], from_mate.at[q], mate_send.at[q], mate_recv.at[q], dev=mate
        )

    def chip_copy(q, k):
        return remote(
            chip_sum.at[q, flip_bits(chip, k)], from_chip.at[q, k - 1],
            chip_send.at[q, k - 1], chip_recv.at[q, k - 1], dev=peer(k),
        )

    def site_copy(q, k):
        return remote(
            sent.at[q], from_site.at[q, k - 1],
            site_send.at[q, k - 1], site_recv.at[q, k - 1], site=other_site(k),
        )

    def row_copy(q, k):
        to = mate if k == 0 else peer(k)
        return remote(
            new_rows.at[q, me], new_rows.at[q, me], row_send.at[q, k], row_recv.at[q, k], dev=to
        )

    def row_arrival(q, k):
        held = new_rows.at[q, mate if k == 0 else peer(k)]
        return remote(held, held, row_send.at[q, k], row_recv.at[q, k], dev=mate)

    def pass_copy(q, k):
        held = new_rows.at[q, peer(k)]
        return remote(held, held, pass_send.at[q, k - 1], pass_recv.at[q, k - 1], dev=mate)

    def pass_arrival(q, k):
        held = new_rows.at[q, flip_bits(chip, k) * 2 + 1 - core]
        return remote(held, held, pass_send.at[q, k - 1], pass_recv.at[q, k - 1], dev=mate)

    def multiply(q):
        tok_load(q).wait()
        grad = jnp.dot(cotan[...], tok[:, cols(q)], preferred_element_type=f32)
        grad = grad.reshape(chips, 2, rows, span)
        for c in range(2):
            part = grad[:, c]
            part = jnp.concatenate(
                [part[:, :, t * LANES:(t + 1) * LANES] for t in range(tiles)], axis=1
            )
            terms[c, q] = part.astype(bf16)
        mate_copy(q).start()

    def add_mate(q):
        mate_copy(q).wait_recv()
        both = terms[core, q].astype(f32) + from_mate[q].astype(f32)
        chip_sum[q] = both.astype(bf16)
        for k in order:
            chip_copy(q, k).start()

    def make_mask():
        index_load.wait()
        held = index[...]
        one = jnp.int32(1)
        low = jnp.sum(jnp.where(held < 32, one << (held & 31), 0), axis=1)
        high = jnp.sum(jnp.where(held >= 32, one << (held & 31), 0), axis=1)
        lane = lax.broadcasted_iota(jnp.int32, (rows, LANES), 1)
        first = lane < SPAN
        lower = (lane % SPAN) < 32
        shift = lane % 32
        for t in range(width // LANES):
            def word(block):
                return jnp.where(
                    lower,
                    jnp.broadcast_to(low[:, block:block + 1], (rows, LANES)),
                    jnp.broadcast_to(high[:, block:block + 1], (rows, LANES)),
                )
            words = jnp.where(first, word(2 * t), word(2 * t + 1))
            mask[t * rows:(t + 1) * rows, :] = ((words >> shift) & 1).astype(f32)

    def pick(q):
        for k in order:
            chip_copy(q, k).wait_recv()
        grad = terms[core, q, chip].astype(f32) + from_mate[q, chip].astype(f32)
        for k in order:
            grad = grad + from_chip[q, k - 1].astype(f32)
        raised = momentum_decay * stack(mom[:, cols(q)]) + grad
        picked = split_dot(raised, table[0]) * mask[pl.ds(pl.multiple_of(q * tiles * rows, tiles * rows), tiles * rows), :]
        sent[q] = picked.astype(bf16)
        for k in range(1, n_site):
            site_copy(q, k).start()
        kept = raised - split_dot(picked, table[1])
        mom_out[0, :, cols(q)] = unstack(kept, rows)

    def update(q):
        for k in range(1, n_site):
            site_copy(q, k).wait_recv()
        total = sent[q].astype(f32)
        for k in range(1, n_site):
            total = total + from_site[q, k - 1].astype(f32)
        decoded = split_dot(total, table[1])
        new_rows[q, me] = (
            stack(weight[:, cols(q)].astype(f32)) - step_size * decoded
        ).astype(bf16)
        for k in order:
            row_copy(q, k).start()
        row_copy(q, 0).start()

    def hand_on(q):
        for k in range(1, chips):
            row_arrival(q, k).wait_recv()
            pass_copy(q, k).start()

    def project(q):
        row_arrival(q, 0).wait_recv()
        for k in range(1, chips):
            pass_arrival(q, k).wait_recv()
        held = new_rows[q].astype(f32)
        held = jnp.concatenate(
            [held[:, t * rows:(t + 1) * rows, :].reshape(n_dev * rows, LANES) for t in range(tiles)],
            axis=1,
        ).astype(bf16)
        total_scores[...] += lax.dot_general(
            held, tok[:, cols(q)], (((1,), (1,)), ((), ())), preferred_element_type=f32
        )

    def each(count, body):
        def step(at, carry):
            body(at)
            return carry
        lax.fori_loop(0, count, step, 0)

    def staggered(step):
        for stage, shift in ((pick, 0), (update, 2), (hand_on, 4), (project, 5)):
            @pl.when((step >= shift) & (step < shift + CHUNKS))
            def _():
                stage(step - shift)

    total_scores[...] = jnp.zeros(total_scores.shape, f32)
    cotan_load.wait()
    pl.semaphore_wait(barrier, chips + n_site - 1)
    each(CHUNKS, multiply)
    each(CHUNKS, add_mate)
    make_mask()
    mom_load.wait()
    table_load.wait()
    weight_load.wait()
    each(CHUNKS + 5, staggered)
    score_out[0] = total_scores[...].astype(bf16)

    def drain(q):
        mate_copy(q).wait_send()
        for k in range(1, chips):
            chip_copy(q, k).wait_send()
            row_copy(q, k).wait_send()
            pass_copy(q, k).wait_send()
        row_copy(q, 0).wait_send()
        for k in range(1, n_site):
            site_copy(q, k).wait_send()

    each(CHUNKS, drain)


def shards(n_dev, n_site, tokens, cotangent, weight, momentum, kept_index):
    count, width = tokens.shape[1:]
    out_rows = cotangent.shape[2]
    rows = weight.shape[0]
    chips = n_dev // 2
    high = rows * width // LANES // CHUNKS
    tables = pair_tables()
    vmem = pl.BlockSpec(memory_space=pltpu.VMEM)
    hbm = pl.BlockSpec(memory_space=pltpu.HBM)
    sems = pltpu.SemaphoreType.DMA
    kept = kept_index.shape[3]
    scores, momentum_new = pl.pallas_call(
        functools.partial(kernel, n_dev, n_site),
        out_shape=(
            pltpu.VMEM((1, out_rows, count), bf16),
            pltpu.VMEM(momentum.shape, f32),
        ),
        in_specs=[hbm] * 6,
        out_specs=(vmem, vmem),
        scratch_shapes=[
            pltpu.VMEM((out_rows, count), bf16),
            pltpu.VMEM((rows, width), bf16),
            pltpu.VMEM(tables.shape, bf16),
            pltpu.VMEM((count, width), bf16),
            pltpu.VMEM((rows, width), f32),
            pltpu.VMEM((rows, kept, width // SPAN), jnp.int32),
            pltpu.VMEM((high * CHUNKS, LANES), f32),
            pltpu.VMEM((out_rows, count), f32),
            pltpu.VMEM((2, CHUNKS, chips, high, LANES), bf16),
            pltpu.VMEM((CHUNKS, chips, high, LANES), bf16),
            pltpu.VMEM((CHUNKS, chips, high, LANES), bf16),
            pltpu.VMEM((CHUNKS, chips - 1, high, LANES), bf16),
            pltpu.VMEM((CHUNKS, high, LANES), bf16),
            pltpu.VMEM((CHUNKS, n_site - 1, high, LANES), bf16),
            pltpu.VMEM((CHUNKS, n_dev, high, LANES), bf16),
            sems, sems, sems, sems((CHUNKS,)), sems, sems,
            sems((CHUNKS,)), sems((CHUNKS,)),
            sems((CHUNKS, chips - 1)), sems((CHUNKS, chips - 1)),
            sems((CHUNKS, n_site - 1)), sems((CHUNKS, n_site - 1)),
            sems((CHUNKS, chips)), sems((CHUNKS, chips)),
            sems((CHUNKS, chips - 1)), sems((CHUNKS, chips - 1)),
        ],
        compiler_params=pltpu.CompilerParams(
            collective_id=0, has_side_effects=True, vmem_limit_bytes=56 * 1024 * 1024
        ),
        cost_estimate=pl.CostEstimate(
            flops=4 * count * width * out_rows, bytes_accessed=4 * count * width, transcendentals=0
        ),
    )(
        tokens,
        cotangent[0].T,
        weight,
        momentum,
        kept_index.transpose(0, 1, 3, 2),
        jnp.asarray(tables),
    )
    return scores.transpose(0, 2, 1), momentum_new


def solution(mesh):
    placed = (
        P("site", "dev", None),
        P("site", "dev", None),
        P("dev", None),
        P("site", "dev", None),
        P(None, "dev", None, None),
    )
    return jax.shard_map(
        functools.partial(shards, mesh.shape["dev"], mesh.shape["site"]),
        mesh=mesh,
        in_specs=placed,
        out_specs=(P("site", "dev", None), P("site", "dev", None)),
        check_vma=False,
    )
```

```python
import functools

import jax
import jax.numpy as jnp
import ml_dtypes
import numpy as np
from jax import lax
from jax.experimental import pallas as pl
from jax.experimental.pallas import tpu as pltpu
from jax.sharding import PartitionSpec as P

momentum_decay = 0.999
step_size = 0.01
SPAN = 64
LANES = 128
CHUNKS = 4
MESH = pl.DeviceIdType.MESH
f32 = jnp.float32
bf16 = jnp.bfloat16


def split_table(table):
    high = table.astype(ml_dtypes.bfloat16)
    low = (table - high.astype(np.float64)).astype(ml_dtypes.bfloat16)
    return np.concatenate([high, high, low], axis=0)


def pair_tables():
    freq = np.arange(SPAN)[:, None]
    place = np.arange(SPAN)[None, :]
    factor = np.where(freq == 0, np.sqrt(1.0 / SPAN), np.sqrt(2.0 / SPAN))
    one = factor * np.cos(np.pi * (2 * place + 1) * freq / (2 * SPAN))
    pair = np.kron(np.eye(LANES // SPAN), one)
    return np.stack([split_table(pair.T), split_table(pair)])


def split_dot(field, factor):
    high = field.astype(bf16)
    low = (field - high.astype(f32)).astype(bf16)
    return jnp.dot(jnp.concatenate([high, low, high], axis=1), factor, preferred_element_type=f32)


def stack(field):
    return jnp.concatenate(
        [field[:, t * LANES:(t + 1) * LANES] for t in range(field.shape[1] // LANES)], axis=0
    )


def unstack(field, rows):
    return jnp.concatenate(
        [field[t * rows:(t + 1) * rows] for t in range(field.shape[0] // rows)], axis=1
    )


def flip_bits(index, bits):
    for power in range(bits.bit_length()):
        if (bits >> power) & 1:
            one = 1 << power
            index = index + one - 2 * one * ((index // one) % 2)
    return index


def kernel(
    n_dev, n_site,
    tok_hbm, cotan_hbm, weight_hbm, mom_hbm, index_hbm, table_hbm,
    score_out, mom_out,
    cotan, weight, table, tok, mom, index, mask, total_scores, terms, from_mate, chip_sum, from_chip, sent, from_site, new_rows,
    cotan_sem, weight_sem, table_sem, tok_sem, mom_sem, index_sem,
    mate_send, mate_recv, chip_send, chip_recv, site_send, site_recv,
    row_send, row_recv, pass_send, pass_recv,
):
    chips = n_dev // 2
    rows, width = mom.shape
    span = width // CHUNKS
    tiles = span // LANES
    me = lax.axis_index("dev")
    site = lax.axis_index("site")
    chip, core = me // 2, me % 2
    mate = chip * 2 + 1 - core
    order = range(chips - 1, 0, -1)

    def peer(k):
        return flip_bits(chip, k) * 2 + core

    def other_site(k):
        return (site + k) % n_site

    barrier = pltpu.get_barrier_semaphore()
    pl.semaphore_signal(barrier, inc=1, device_id={"dev": mate}, device_id_type=MESH)
    for k in order:
        pl.semaphore_signal(barrier, inc=1, device_id={"dev": peer(k)}, device_id_type=MESH)
    for k in range(1, n_site):
        pl.semaphore_signal(barrier, inc=1, device_id={"site": other_site(k)}, device_id_type=MESH)

    def cols(q):
        return pl.ds(pl.multiple_of(q * span, span), span)

    def tok_load(q):
        return pltpu.make_async_copy(tok_hbm.at[0, :, cols(q)], tok.at[:, cols(q)], tok_sem.at[q])

    index_load = pltpu.make_async_copy(index_hbm.at[site], index, index_sem)
    index_load.start()
    cotan_load = pltpu.make_async_copy(cotan_hbm, cotan, cotan_sem)
    weight_load = pltpu.make_async_copy(weight_hbm, weight, weight_sem)
    table_load = pltpu.make_async_copy(table_hbm, table, table_sem)
    cotan_load.start()
    for q in range(CHUNKS):
        tok_load(q).start()
    mom_load = pltpu.make_async_copy(mom_hbm.at[0], mom, mom_sem)
    mom_load.start()
    table_load.start()
    weight_load.start()

    def remote(src, dst, send_sem, recv_sem, **where):
        return pltpu.make_async_remote_copy(
            src_ref=src, dst_ref=dst, send_sem=send_sem, recv_sem=recv_sem,
            device_id=where, device_id_type=MESH,
        )

    def mate_copy(q):
        return remote(
            terms.at[1 - core, q], from_mate.at[q], mate_send.at[q], mate_recv.at[q], dev=mate
        )

    def chip_copy(q, k):
        return remote(
            chip_sum.at[q, flip_bits(chip, k)], from_chip.at[q, k - 1],
            chip_send.at[q, k - 1], chip_recv.at[q, k - 1], dev=peer(k),
        )

    def site_copy(q, k):
        return remote(
            sent.at[q], from_site.at[q, k - 1],
            site_send.at[q, k - 1], site_recv.at[q, k - 1], site=other_site(k),
        )

    def row_copy(q, k):
        to = mate if k == 0 else peer(k)
        return remote(
            new_rows.at[q, me], new_rows.at[q, me], row_send.at[q, k], row_recv.at[q, k], dev=to
        )

    def row_arrival(q, k):
        held = new_rows.at[q, mate if k == 0 else peer(k)]
        return remote(held, held, row_send.at[q, k], row_recv.at[q, k], dev=mate)

    def pass_copy(q, k):
        held = new_rows.at[q, peer(k)]
        return remote(held, held, pass_send.at[q, k - 1], pass_recv.at[q, k - 1], dev=mate)

    def pass_arrival(q, k):
        held = new_rows.at[q, flip_bits(chip, k) * 2 + 1 - core]
        return remote(held, held, pass_send.at[q, k - 1], pass_recv.at[q, k - 1], dev=mate)

    def multiply(q):
        tok_load(q).wait()
        grad = jnp.dot(cotan[...], tok[:, cols(q)], preferred_element_type=f32)
        grad = grad.reshape(chips, 2, rows, span)
        for c in range(2):
            part = grad[:, c]
            part = jnp.concatenate(
                [part[:, :, t * LANES:(t + 1) * LANES] for t in range(tiles)], axis=1
            )
            terms[c, q] = part.astype(bf16)

        @pl.when(q == 0)
        def _():
            pl.semaphore_wait(barrier, chips + n_site - 1)
        mate_copy(q).start()

    def add_mate(q):
        mate_copy(q).wait_recv()
        both = terms[core, q].astype(f32) + from_mate[q].astype(f32)
        chip_sum[q] = both.astype(bf16)
        for k in order:
            chip_copy(q, k).start()

    def make_mask():
        index_load.wait()
        held = index[...]
        one = jnp.int32(1)
        low = jnp.sum(jnp.where(held < 32, one << (held & 31), 0), axis=1)
        high = jnp.sum(jnp.where(held >= 32, one << (held & 31), 0), axis=1)
        lane = lax.broadcasted_iota(jnp.int32, (rows, LANES), 1)
        first = lane < SPAN
        lower = (lane % SPAN) < 32
        shift = lane % 32
        for t in range(width // LANES):
            def word(block):
                return jnp.where(
                    lower,
                    jnp.broadcast_to(low[:, block:block + 1], (rows, LANES)),
                    jnp.broadcast_to(high[:, block:block + 1], (rows, LANES)),
                )
            words = jnp.where(first, word(2 * t), word(2 * t + 1))
            mask[t * rows:(t + 1) * rows, :] = ((words >> shift) & 1).astype(f32)

    def pick(q):
        for k in order:
            chip_copy(q, k).wait_recv()
        grad = terms[core, q, chip].astype(f32) + from_mate[q, chip].astype(f32)
        for k in order:
            grad = grad + from_chip[q, k - 1].astype(f32)
        raised = momentum_decay * stack(mom[:, cols(q)]) + grad
        picked = split_dot(raised, table[0]) * mask[pl.ds(pl.multiple_of(q * tiles * rows, tiles * rows), tiles * rows), :]
        sent[q] = picked.astype(bf16)
        for k in range(1, n_site):
            site_copy(q, k).start()
        kept = raised - split_dot(picked, table[1])
        mom_out[0, :, cols(q)] = unstack(kept, rows)

    def update(q):
        for k in range(1, n_site):
            site_copy(q, k).wait_recv()
        total = sent[q].astype(f32)
        for k in range(1, n_site):
            total = total + from_site[q, k - 1].astype(f32)
        decoded = split_dot(total, table[1])
        new_rows[q, me] = (
            stack(weight[:, cols(q)].astype(f32)) - step_size * decoded
        ).astype(bf16)
        for k in order:
            row_copy(q, k).start()
        row_copy(q, 0).start()

    def hand_on(q):
        for k in range(1, chips):
            row_arrival(q, k).wait_recv()
            pass_copy(q, k).start()

    def project(q):
        row_arrival(q, 0).wait_recv()
        for k in range(1, chips):
            pass_arrival(q, k).wait_recv()
        held = new_rows[q].astype(f32)
        held = jnp.concatenate(
            [held[:, t * rows:(t + 1) * rows, :].reshape(n_dev * rows, LANES) for t in range(tiles)],
            axis=1,
        ).astype(bf16)
        total_scores[...] += lax.dot_general(
            held, tok[:, cols(q)], (((1,), (1,)), ((), ())), preferred_element_type=f32
        )

    def each(count, body):
        def step(at, carry):
            body(at)
            return carry
        lax.fori_loop(0, count, step, 0)

    def staggered(step):
        for stage, shift in ((pick, 0), (update, 2), (hand_on, 4), (project, 5)):
            @pl.when((step >= shift) & (step < shift + CHUNKS))
            def _():
                stage(step - shift)

    total_scores[...] = jnp.zeros(total_scores.shape, f32)
    make_mask()
    cotan_load.wait()
    each(CHUNKS, multiply)
    each(CHUNKS, add_mate)
    mom_load.wait()
    table_load.wait()
    weight_load.wait()
    each(CHUNKS + 5, staggered)
    score_out[0] = total_scores[...].astype(bf16)

    def drain(q):
        mate_copy(q).wait_send()
        for k in range(1, chips):
            chip_copy(q, k).wait_send()
            row_copy(q, k).wait_send()
            pass_copy(q, k).wait_send()
        row_copy(q, 0).wait_send()
        for k in range(1, n_site):
            site_copy(q, k).wait_send()

    each(CHUNKS, drain)


def shards(n_dev, n_site, tokens, cotangent, weight, momentum, kept_index):
    count, width = tokens.shape[1:]
    out_rows = cotangent.shape[2]
    rows = weight.shape[0]
    chips = n_dev // 2
    high = rows * width // LANES // CHUNKS
    tables = pair_tables()
    vmem = pl.BlockSpec(memory_space=pltpu.VMEM)
    hbm = pl.BlockSpec(memory_space=pltpu.HBM)
    sems = pltpu.SemaphoreType.DMA
    kept = kept_index.shape[3]
    scores, momentum_new = pl.pallas_call(
        functools.partial(kernel, n_dev, n_site),
        out_shape=(
            pltpu.VMEM((1, out_rows, count), bf16),
            pltpu.VMEM(momentum.shape, f32),
        ),
        in_specs=[hbm] * 6,
        out_specs=(vmem, vmem),
        scratch_shapes=[
            pltpu.VMEM((out_rows, count), bf16),
            pltpu.VMEM((rows, width), bf16),
            pltpu.VMEM(tables.shape, bf16),
            pltpu.VMEM((count, width), bf16),
            pltpu.VMEM((rows, width), f32),
            pltpu.VMEM((rows, kept, width // SPAN), jnp.int32),
            pltpu.VMEM((high * CHUNKS, LANES), f32),
            pltpu.VMEM((out_rows, count), f32),
            pltpu.VMEM((2, CHUNKS, chips, high, LANES), bf16),
            pltpu.VMEM((CHUNKS, chips, high, LANES), bf16),
            pltpu.VMEM((CHUNKS, chips, high, LANES), bf16),
            pltpu.VMEM((CHUNKS, chips - 1, high, LANES), bf16),
            pltpu.VMEM((CHUNKS, high, LANES), bf16),
            pltpu.VMEM((CHUNKS, n_site - 1, high, LANES), bf16),
            pltpu.VMEM((CHUNKS, n_dev, high, LANES), bf16),
            sems, sems, sems, sems((CHUNKS,)), sems, sems,
            sems((CHUNKS,)), sems((CHUNKS,)),
            sems((CHUNKS, chips - 1)), sems((CHUNKS, chips - 1)),
            sems((CHUNKS, n_site - 1)), sems((CHUNKS, n_site - 1)),
            sems((CHUNKS, chips)), sems((CHUNKS, chips)),
            sems((CHUNKS, chips - 1)), sems((CHUNKS, chips - 1)),
        ],
        compiler_params=pltpu.CompilerParams(
            collective_id=0, has_side_effects=True, vmem_limit_bytes=56 * 1024 * 1024
        ),
        cost_estimate=pl.CostEstimate(
            flops=4 * count * width * out_rows, bytes_accessed=4 * count * width, transcendentals=0
        ),
    )(
        tokens,
        cotangent[0].T,
        weight,
        momentum,
        kept_index.transpose(0, 1, 3, 2),
        jnp.asarray(tables),
    )
    return scores.transpose(0, 2, 1), momentum_new


def solution(mesh):
    placed = (
        P("site", "dev", None),
        P("site", "dev", None),
        P("dev", None),
        P("site", "dev", None),
        P(None, "dev", None, None),
    )
    return jax.shard_map(
        functools.partial(shards, mesh.shape["dev"], mesh.shape["site"]),
        mesh=mesh,
        in_specs=placed,
        out_specs=(P("site", "dev", None), P("site", "dev", None)),
        check_vma=False,
    )
```

```python
import functools

import jax
import jax.numpy as jnp
import ml_dtypes
import numpy as np
from jax import lax
from jax.experimental import pallas as pl
from jax.experimental.pallas import tpu as pltpu
from jax.sharding import PartitionSpec as P

momentum_decay = 0.999
step_size = 0.01
SPAN = 64
LANES = 128
CHUNKS = 4
MESH = pl.DeviceIdType.MESH
f32 = jnp.float32
bf16 = jnp.bfloat16


def split_table(table):
    high = table.astype(ml_dtypes.bfloat16)
    low = (table - high.astype(np.float64)).astype(ml_dtypes.bfloat16)
    return np.concatenate([high, high, low], axis=0)


def pair_tables():
    freq = np.arange(SPAN)[:, None]
    place = np.arange(SPAN)[None, :]
    factor = np.where(freq == 0, np.sqrt(1.0 / SPAN), np.sqrt(2.0 / SPAN))
    one = factor * np.cos(np.pi * (2 * place + 1) * freq / (2 * SPAN))
    pair = np.kron(np.eye(LANES // SPAN), one)
    return np.stack([split_table(pair.T), split_table(pair)])


def split_dot(field, factor):
    high = field.astype(bf16)
    low = (field - high.astype(f32)).astype(bf16)
    return jnp.dot(jnp.concatenate([high, low, high], axis=1), factor, preferred_element_type=f32)


def stack(field):
    return jnp.concatenate(
        [field[:, t * LANES:(t + 1) * LANES] for t in range(field.shape[1] // LANES)], axis=0
    )


def unstack(field, rows):
    return jnp.concatenate(
        [field[t * rows:(t + 1) * rows] for t in range(field.shape[0] // rows)], axis=1
    )


def flip_bits(index, bits):
    for power in range(bits.bit_length()):
        if (bits >> power) & 1:
            one = 1 << power
            index = index + one - 2 * one * ((index // one) % 2)
    return index


def kernel(
    n_dev, n_site,
    tok_hbm, cotan_hbm, weight_hbm, mom_hbm, index_hbm, table_hbm,
    score_out, mom_out,
    cotan, weight, table, tok, mom, index, mask, total_scores, terms, from_mate, chip_sum, from_chip, sent, from_site, new_rows,
    cotan_sem, weight_sem, table_sem, tok_sem, mom_sem, index_sem,
    mate_send, mate_recv, chip_send, chip_recv, site_send, site_recv,
    row_send, row_recv, pass_send, pass_recv,
):
    chips = n_dev // 2
    rows, width = mom.shape
    span = width // CHUNKS
    tiles = span // LANES
    me = lax.axis_index("dev")
    site = lax.axis_index("site")
    chip, core = me // 2, me % 2
    mate = chip * 2 + 1 - core
    order = range(chips - 1, 0, -1)

    def peer(k):
        return flip_bits(chip, k) * 2 + core

    def other_site(k):
        return (site + k) % n_site

    barrier = pltpu.get_barrier_semaphore()
    pl.semaphore_signal(barrier, inc=1, device_id={"dev": mate}, device_id_type=MESH)
    for k in order:
        pl.semaphore_signal(barrier, inc=1, device_id={"dev": peer(k)}, device_id_type=MESH)
    for k in range(1, n_site):
        pl.semaphore_signal(barrier, inc=1, device_id={"site": other_site(k)}, device_id_type=MESH)

    def cols(q):
        return pl.ds(pl.multiple_of(q * span, span), span)

    def tok_load(q):
        return pltpu.make_async_copy(tok_hbm.at[0, :, cols(q)], tok.at[:, cols(q)], tok_sem.at[q])

    cotan_load = pltpu.make_async_copy(cotan_hbm, cotan, cotan_sem)
    weight_load = pltpu.make_async_copy(weight_hbm, weight, weight_sem)
    table_load = pltpu.make_async_copy(table_hbm, table, table_sem)
    cotan_load.start()
    for q in range(CHUNKS):
        tok_load(q).start()
    index_load = pltpu.make_async_copy(index_hbm.at[site], index, index_sem)
    index_load.start()
    mom_load = pltpu.make_async_copy(mom_hbm.at[0], mom, mom_sem)
    mom_load.start()
    table_load.start()
    weight_load.start()

    def remote(src, dst, send_sem, recv_sem, **where):
        return pltpu.make_async_remote_copy(
            src_ref=src, dst_ref=dst, send_sem=send_sem, recv_sem=recv_sem,
            device_id=where, device_id_type=MESH,
        )

    def mate_copy(q):
        return remote(
            terms.at[1 - core, q], from_mate.at[q], mate_send.at[q], mate_recv.at[q], dev=mate
        )

    def chip_copy(q, k):
        return remote(
            chip_sum.at[q, flip_bits(chip, k)], from_chip.at[q, k - 1],
            chip_send.at[q, k - 1], chip_recv.at[q, k - 1], dev=peer(k),
        )

    def site_copy(q, k):
        return remote(
            sent.at[q], from_site.at[q, k - 1],
            site_send.at[q, k - 1], site_recv.at[q, k - 1], site=other_site(k),
        )

    def row_copy(q, k):
        to = mate if k == 0 else peer(k)
        return remote(
            new_rows.at[q, me], new_rows.at[q, me], row_send.at[q, k], row_recv.at[q, k], dev=to
        )

    def row_arrival(q, k):
        held = new_rows.at[q, mate if k == 0 else peer(k)]
        return remote(held, held, row_send.at[q, k], row_recv.at[q, k], dev=mate)

    def pass_copy(q, k):
        held = new_rows.at[q, peer(k)]
        return remote(held, held, pass_send.at[q, k - 1], pass_recv.at[q, k - 1], dev=mate)

    def pass_arrival(q, k):
        held = new_rows.at[q, flip_bits(chip, k) * 2 + 1 - core]
        return remote(held, held, pass_send.at[q, k - 1], pass_recv.at[q, k - 1], dev=mate)

    def multiply(q):
        tok_load(q).wait()
        grad = jnp.dot(cotan[...], tok[:, cols(q)], preferred_element_type=f32)
        grad = grad.reshape(chips, 2, rows, span)
        for c in range(2):
            part = grad[:, c]
            part = jnp.concatenate(
                [part[:, :, t * LANES:(t + 1) * LANES] for t in range(tiles)], axis=1
            )
            terms[c, q] = part.astype(bf16)
        mate_copy(q).start()

    def add_mate(q):
        mate_copy(q).wait_recv()
        both = terms[core, q].astype(f32) + from_mate[q].astype(f32)
        chip_sum[q] = both.astype(bf16)
        for k in order:
            chip_copy(q, k).start()

    def mask_words():
        index_load.wait()
        held = index[...]
        one = jnp.int32(1)
        low = jnp.sum(jnp.where(held < 32, one << (held & 31), 0), axis=1)
        high = jnp.sum(jnp.where(held >= 32, one << (held & 31), 0), axis=1)
        return low, high

    def make_mask(q, low, high):
        lane = lax.broadcasted_iota(jnp.int32, (rows, LANES), 1)
        first = lane < SPAN
        lower = (lane % SPAN) < 32
        shift = lane % 32
        for t in range(q * tiles, (q + 1) * tiles):
            def word(block):
                return jnp.where(
                    lower,
                    jnp.broadcast_to(low[:, block:block + 1], (rows, LANES)),
                    jnp.broadcast_to(high[:, block:block + 1], (rows, LANES)),
                )
            words = jnp.where(first, word(2 * t), word(2 * t + 1))
            mask[t * rows:(t + 1) * rows, :] = ((words >> shift) & 1).astype(f32)

    def pick(q):
        for k in order:
            chip_copy(q, k).wait_recv()
        grad = terms[core, q, chip].astype(f32) + from_mate[q, chip].astype(f32)
        for k in order:
            grad = grad + from_chip[q, k - 1].astype(f32)
        raised = momentum_decay * stack(mom[:, cols(q)]) + grad
        picked = split_dot(raised, table[0]) * mask[pl.ds(pl.multiple_of(q * tiles * rows, tiles * rows), tiles * rows), :]
        sent[q] = picked.astype(bf16)
        for k in range(1, n_site):
            site_copy(q, k).start()
        kept = raised - split_dot(picked, table[1])
        mom_out[0, :, cols(q)] = unstack(kept, rows)

    def update(q):
        for k in range(1, n_site):
            site_copy(q, k).wait_recv()
        total = sent[q].astype(f32)
        for k in range(1, n_site):
            total = total + from_site[q, k - 1].astype(f32)
        decoded = split_dot(total, table[1])
        new_rows[q, me] = (
            stack(weight[:, cols(q)].astype(f32)) - step_size * decoded
        ).astype(bf16)
        for k in order:
            row_copy(q, k).start()
        row_copy(q, 0).start()

    def hand_on(q):
        for k in range(1, chips):
            row_arrival(q, k).wait_recv()
            pass_copy(q, k).start()

    def project(q):
        row_arrival(q, 0).wait_recv()
        for k in range(1, chips):
            pass_arrival(q, k).wait_recv()
        held = new_rows[q].astype(f32)
        held = jnp.concatenate(
            [held[:, t * rows:(t + 1) * rows, :].reshape(n_dev * rows, LANES) for t in range(tiles)],
            axis=1,
        ).astype(bf16)
        total_scores[...] += lax.dot_general(
            held, tok[:, cols(q)], (((1,), (1,)), ((), ())), preferred_element_type=f32
        )

    def each(count, body):
        def step(at, carry):
            body(at)
            return carry
        lax.fori_loop(0, count, step, 0)

    def staggered(step):
        for q in range(1, CHUNKS):
            @pl.when(step == q)
            def _():
                make_mask(q, low, high)
        for stage, shift in ((pick, 0), (update, 2), (hand_on, 4), (project, 5)):
            @pl.when((step >= shift) & (step < shift + CHUNKS))
            def _():
                stage(step - shift)

    total_scores[...] = jnp.zeros(total_scores.shape, f32)
    cotan_load.wait()
    pl.semaphore_wait(barrier, chips + n_site - 1)
    each(CHUNKS, multiply)
    each(CHUNKS, add_mate)
    low, high = mask_words()
    make_mask(0, low, high)
    mom_load.wait()
    table_load.wait()
    weight_load.wait()
    each(CHUNKS + 5, staggered)
    score_out[0] = total_scores[...].astype(bf16)

    def drain(q):
        mate_copy(q).wait_send()
        for k in range(1, chips):
            chip_copy(q, k).wait_send()
            row_copy(q, k).wait_send()
            pass_copy(q, k).wait_send()
        row_copy(q, 0).wait_send()
        for k in range(1, n_site):
            site_copy(q, k).wait_send()

    each(CHUNKS, drain)


def shards(n_dev, n_site, tokens, cotangent, weight, momentum, kept_index):
    count, width = tokens.shape[1:]
    out_rows = cotangent.shape[2]
    rows = weight.shape[0]
    chips = n_dev // 2
    high = rows * width // LANES // CHUNKS
    tables = pair_tables()
    vmem = pl.BlockSpec(memory_space=pltpu.VMEM)
    hbm = pl.BlockSpec(memory_space=pltpu.HBM)
    sems = pltpu.SemaphoreType.DMA
    kept = kept_index.shape[3]
    scores, momentum_new = pl.pallas_call(
        functools.partial(kernel, n_dev, n_site),
        out_shape=(
            pltpu.VMEM((1, out_rows, count), bf16),
            pltpu.VMEM(momentum.shape, f32),
        ),
        in_specs=[hbm] * 6,
        out_specs=(vmem, vmem),
        scratch_shapes=[
            pltpu.VMEM((out_rows, count), bf16),
            pltpu.VMEM((rows, width), bf16),
            pltpu.VMEM(tables.shape, bf16),
            pltpu.VMEM((count, width), bf16),
            pltpu.VMEM((rows, width), f32),
            pltpu.VMEM((rows, kept, width // SPAN), jnp.int32),
            pltpu.VMEM((high * CHUNKS, LANES), f32),
            pltpu.VMEM((out_rows, count), f32),
            pltpu.VMEM((2, CHUNKS, chips, high, LANES), bf16),
            pltpu.VMEM((CHUNKS, chips, high, LANES), bf16),
            pltpu.VMEM((CHUNKS, chips, high, LANES), bf16),
            pltpu.VMEM((CHUNKS, chips - 1, high, LANES), bf16),
            pltpu.VMEM((CHUNKS, high, LANES), bf16),
            pltpu.VMEM((CHUNKS, n_site - 1, high, LANES), bf16),
            pltpu.VMEM((CHUNKS, n_dev, high, LANES), bf16),
            sems, sems, sems, sems((CHUNKS,)), sems, sems,
            sems((CHUNKS,)), sems((CHUNKS,)),
            sems((CHUNKS, chips - 1)), sems((CHUNKS, chips - 1)),
            sems((CHUNKS, n_site - 1)), sems((CHUNKS, n_site - 1)),
            sems((CHUNKS, chips)), sems((CHUNKS, chips)),
            sems((CHUNKS, chips - 1)), sems((CHUNKS, chips - 1)),
        ],
        compiler_params=pltpu.CompilerParams(
            collective_id=0, has_side_effects=True, vmem_limit_bytes=56 * 1024 * 1024
        ),
        cost_estimate=pl.CostEstimate(
            flops=4 * count * width * out_rows, bytes_accessed=4 * count * width, transcendentals=0
        ),
    )(
        tokens,
        cotangent[0].T,
        weight,
        momentum,
        kept_index.transpose(0, 1, 3, 2),
        jnp.asarray(tables),
    )
    return scores.transpose(0, 2, 1), momentum_new


def solution(mesh):
    placed = (
        P("site", "dev", None),
        P("site", "dev", None),
        P("dev", None),
        P("site", "dev", None),
        P(None, "dev", None, None),
    )
    return jax.shard_map(
        functools.partial(shards, mesh.shape["dev"], mesh.shape["site"]),
        mesh=mesh,
        in_specs=placed,
        out_specs=(P("site", "dev", None), P("site", "dev", None)),
        check_vma=False,
    )
```
